32 devices in a mesh: groups: 2 (over y), cells: 4 (over z), role: 2 (over x), stack: 2 (over core).
Axes of the slice: x: 2, y: 2, z: 4, core: 2. Of those that a mesh axis runs over, the one named last changes fastest.
Arguments:
- height: float32 [90, 49152], P('stack', ('groups', 'cells', 'role')), parts along dimension 1, may hold values from -6 to 6
- velocity: float32 [90, 73728], P('stack', ('groups', 'cells', 'role')), parts along dimension 1, may hold values from -6 to 6
- tracers: bfloat16 [6, 90, 49152], P(None, 'stack', ('groups', 'cells', 'role')), parts along dimension 2, may hold values from -6 to 6
- edge_coef: float32 [36864], P(('cells', 'role')), may hold values from 0.1 to 0.6
- cell_coef: float32 [3, 24576], P(None, ('cells', 'role')), may hold values from -2.5 to 2.5
- halo_send: int32 [8, 512], P(('cells', 'role')), may hold values from 0 to 3071
- edge_cells: int32 [8, 2, 4608], P(('cells', 'role')), may hold values from 0 to 3583
- cell_edges: int32 [8, 3, 3072], P(('cells', 'role')), may hold values from 0 to 4607
- send_block: int32 [8, 16], P(('cells', 'role')), may hold values from -1 to 23, as said below
- recv_slot: int32 [8, 8], P(('cells', 'role')), may hold values from 0 to 15, as said below
- block_count: int32 [8, 24], P(('cells', 'role')), may hold values from 1 to 128
- w_first: bfloat16 [900, 512], P('stack'), may hold values from -0.1875 to 0.1875
- b_first: bfloat16 [512], replicated, may hold values from -3 to 3
- w_second: bfloat16 [512, 512], P(None, 'stack'), may hold values from -0.25 to 0.25
- b_second: bfloat16 [512], P('stack'), may hold values from -3 to 3
- w_third: bfloat16 [512, 90], P('stack'), may hold values from -0.25 to 0.25
Outputs:
- height_out: float32 [90, 49152], P('stack', ('groups', 'cells', 'role')), parts along dimension 1
The draws below stay inside these ranges and needn't reach their ends.
There are 2 independent parts, one for each index of `groups`. The reference program is written for one: setup_inputs(seed, part) draws one part's arguments, and reference() takes and returns one part's arrays. A program takes and returns all parts, laid end to end along the dimension named above; an argument that names none is the same for every part. Nothing has to cross between parts.
Inputs may be any that keep to these rules, and one draw needn't show every extreme that they name: `send_block`: entries are blocks of the domain or -1. Slots c * 4 to c * 4 + 3 go to the domain with cells index c and the same role index. A domain names each block at most once and fills 1 to 16 slots; in every group of domains with one role index, one domain fills exactly 16. `recv_slot`: every domain computes the physics of exactly 8 blocks; entry s names the incoming slot (s // 4 is the sender's cells index), and the sender's slot it names is filled. The entries of one domain are distinct.
All inputs are finite; a program needn't handle non-finite values.
Results may differ from the reference program's by a relative error of at most 0.0012.
Values may be sent and summed in bfloat16 or wider, within the bound.
A program may use at most 64 MiB of HBM per device.

```python
import math
import jax
import jax.numpy as jnp
from jax import lax

LEV = 90
NQ = 10
HID = 512
BLK = 128
NB = 24
H = 256
FEAT = 900
NTR = 6
C = 3072
E = 4608
NDOM = 8
NCELL = 24576
NEDGE = 36864
RMAX = 8
SLOTS = 16
SMAX = 16
CAP = 4
N_CELLS = 4
N_ROLE = 2


def assignment(key):
    width = N_CELLS
    key_weight, key_busy, key_dest, key_block = jax.random.split(key, 4)
    weights = jax.random.randint(key_weight, (N_ROLE, width), 1, 3)
    busy = jax.random.randint(key_busy, (N_ROLE,), 0, width)
    is_busy = jnp.arange(width)[None, :] == busy[:, None]
    weights = jnp.where(is_busy, 0, weights)
    spare = width * RMAX - SMAX - (width - 1)
    share = spare * weights // jnp.sum(weights, axis=1, keepdims=True)
    left = spare - jnp.sum(share, axis=1, keepdims=True)
    order = jnp.cumsum(jnp.where(is_busy, 0, 1), axis=1) - 1
    extra = jnp.where(is_busy, 0, (order < left).astype(jnp.int32))
    counts = jnp.where(is_busy, SMAX, 1 + share + extra).astype(jnp.int32)
    starts = jnp.cumsum(counts, axis=1) - counts
    dest_order = jax.vmap(lambda k: jax.random.permutation(k, width))(jax.random.split(key_dest, N_ROLE)).astype(jnp.int32)
    block_order = jax.vmap(lambda k: jax.random.permutation(k, NB))(jax.random.split(key_block, NDOM)).astype(jnp.int32)
    return (counts, starts, dest_order, block_order)


def draw_send_block(key, part):
    counts, starts, dest_order, block_order = assignment(key)
    width = N_CELLS
    domains = jnp.arange(NDOM)
    role_of = domains % N_ROLE
    cell_of = domains // N_ROLE
    count_dom = counts[role_of, cell_of]
    start_dom = starts[role_of, cell_of]
    steps = jnp.arange(SMAX)
    live = steps[None, :] < count_dom[:, None]
    item = start_dom[:, None] + steps[None, :]
    dest = dest_order[role_of[:, None], item % width]
    slot = dest * CAP + steps[None, :] // width
    rows = jnp.broadcast_to(domains[:, None], (NDOM, SMAX))
    table = jnp.full((NDOM, SLOTS), -1, jnp.int32)
    return table.at[rows, jnp.where(live, slot, SLOTS)].set(block_order[:, :SMAX], mode='drop')


def draw_recv_slot(key, part):
    counts, starts, dest_order, block_order = assignment(key)
    width = N_CELLS
    domains = jnp.arange(NDOM)
    role_of = domains % N_ROLE
    cell_of = domains // N_ROLE
    inverse = jnp.argsort(dest_order, axis=1)
    place = inverse[role_of, cell_of]
    item = place[:, None] + width * jnp.arange(RMAX)[None, :]
    start_rows = starts[role_of]
    source = jnp.sum((start_rows[:, None, :] <= item[:, :, None]).astype(jnp.int32), axis=2) - 1
    first_item = jnp.take_along_axis(start_rows, source, axis=1)
    return (source * CAP + (item - first_item) // width).astype(jnp.int32)


def plant(array, key, least, largest):
    shape = array.shape
    index_at = [jax.random.randint(jax.random.fold_in(key, axis), (), 0, shape[axis]) for axis in range(len(shape))]
    array = array.at[tuple(index_at)].set(least)
    longest = shape.index(max(shape))
    index_at[longest] = (index_at[longest] + 1) % shape[longest]
    return array.at[tuple(index_at)].set(largest)


def block_levels(own_key, shape, pieces, least, largest):
    def one(dim, blocks):
        heights = jax.random.uniform(jax.random.fold_in(jax.random.fold_in(own_key, 6), dim), (blocks,), jnp.float32, least / len(pieces), largest / len(pieces))
        return jnp.repeat(jnp.exp(heights), shape[dim] // blocks).reshape((-1,) + (1,) * (len(shape) - dim - 1))

    factor_of = one(*pieces[0])
    for cut in pieces[1:]:
        factor_of = factor_of * one(*cut)
    return factor_of


def noise(stream_key, shape, scale, bound, pieces=(), held_as=jnp.bfloat16):
    drawn = jax.random.normal(stream_key, shape, jnp.float32) * scale
    if len(pieces) > 0:
        drawn = block_levels(stream_key, shape, pieces, -0.22, 0.18) * drawn
    return jnp.clip(drawn, min=-bound, max=bound).astype(held_as)


def setup_inputs(seed: int = 0, part: int = 0) -> dict:
    keys = jax.random.split(jax.random.key(seed), 17)
    part_keys = jax.random.split(jax.random.fold_in(keys[16], part), 17)
    return {
        "height": noise(part_keys[0], (LEV, NCELL), 1.0, 6.0, ((0, 2), (1, 8)), jnp.float32),
        "velocity": noise(part_keys[1], (LEV, NEDGE), 1.0, 6.0, ((0, 2), (1, 8)), jnp.float32),
        "tracers": noise(part_keys[2], (NTR, LEV, NCELL), 1.0, 6.0, ((1, 2), (2, 8))),
        "edge_coef": jnp.clip(jnp.exp(math.log(0.6) - 1.7917595 * jax.random.uniform(keys[3], (NEDGE,), jnp.float32) ** block_levels(keys[3], (NEDGE,), ((0, 8),), -0.2, 0.2)), 0.1, 0.6),
        "cell_coef": noise(keys[4], (3, NCELL), 0.4, 2.5, ((1, 8),), jnp.float32),
        "halo_send": plant(jax.random.randint(keys[5], (NDOM, 2 * H), 0, C), jax.random.fold_in(keys[5], 1), 0, C - 1).astype(jnp.int32),
        "edge_cells": plant(jax.random.randint(keys[6], (NDOM, 2, E), 0, C + 2 * H), jax.random.fold_in(keys[6], 1), 0, (C + 2 * H) - 1).astype(jnp.int32),
        "cell_edges": plant(jax.random.randint(keys[7], (NDOM, 3, C), 0, E), jax.random.fold_in(keys[7], 1), 0, E - 1).astype(jnp.int32),
        "send_block": draw_send_block(jax.random.fold_in(keys[16], 71), part),
        "recv_slot": draw_recv_slot(jax.random.fold_in(keys[16], 71), part),
        "block_count": plant(jax.random.randint(keys[10], (NDOM, NB), 1, BLK + 1), jax.random.fold_in(keys[10], 1), 1, BLK).astype(jnp.int32),
        "w_first": noise(keys[11], (FEAT, HID), FEAT ** -0.5, 0.1875, ((0, 2),)),
        "b_first": noise(keys[12], (HID,), 0.5, 3.0),
        "w_second": noise(keys[13], (HID, HID), HID ** -0.5, 0.25, ((1, 2),)),
        "b_second": noise(keys[14], (HID,), 0.5, 3.0, ((0, 2),)),
        "w_third": noise(keys[15], (HID, LEV), HID ** -0.5, 0.25, ((0, 2),)),
    }


def take_cells(field, table):
    return jax.vmap(lambda f, i: jnp.take(f, i, axis=1), in_axes=(1, 0), out_axes=1)(field, table)


def substep(height, velocity, edge_coef, cell_coef, halo_send, edge_cells, cell_edges):
    packed = take_cells(height, halo_send)
    from_prev = jnp.roll(packed[:, :, H:], 1, axis=1)
    from_next = jnp.roll(packed[:, :, :H], -1, axis=1)
    extended = jnp.concatenate([height, from_prev, from_next], axis=2)
    first = take_cells(extended, edge_cells[:, 0])
    second = take_cells(extended, edge_cells[:, 1])
    moved = velocity - edge_coef[None] * (second - first)
    beside_all = jax.vmap(lambda f, i: jnp.take(f, i, axis=1), in_axes=(1, 0), out_axes=2)(moved, cell_edges)
    spread = jnp.sum(cell_coef[None] * beside_all, axis=1)
    return height - spread, moved, spread, beside_all


def reference(height, velocity, tracers, edge_coef, cell_coef, halo_send, edge_cells, cell_edges, send_block, recv_slot, block_count, w_first, b_first, w_second, b_second, w_third):
    cells_now = height.reshape(LEV, NDOM, C)
    edges_now = velocity.reshape(LEV, NDOM, E)
    edge_weight = edge_coef.reshape(NDOM, E)
    cell_weight = cell_coef.reshape(3, NDOM, C)
    first_h, first_v, first_div, beside_all = substep(cells_now, edges_now, edge_weight, cell_weight, halo_send, edge_cells, cell_edges)
    second_h, second_v, second_div, second_around = substep(first_h, first_v, edge_weight, cell_weight, halo_send, edge_cells, cell_edges)
    derived = jnp.stack([first_h, first_div, jnp.mean(beside_all * beside_all, axis=1), jnp.mean(beside_all, axis=1)]).astype(jnp.bfloat16)
    quantities = jnp.concatenate([derived, tracers.reshape(NTR, LEV, NDOM, C)], axis=0)
    features = quantities.reshape(NQ, LEV, NDOM, NB, BLK).transpose(2, 3, 1, 0, 4).reshape(NDOM, NB, FEAT, BLK)
    domains = jnp.arange(NDOM, dtype=jnp.int32)
    role_of = domains % N_ROLE
    cell_of = domains // N_ROLE
    source = (recv_slot // CAP) * N_ROLE + role_of[:, None]
    position = cell_of[:, None] * CAP + recv_slot % CAP
    block = send_block[source, position]
    inputs = features[source, block]
    w_one = w_first.astype(jnp.float32)
    w_two = w_second.astype(jnp.float32)
    w_out = w_third.astype(jnp.float32)
    bias_one = b_first.astype(jnp.float32)[None, :, None]
    bias_two = b_second.astype(jnp.float32)[None, :, None]

    def network(block_inputs):
        pre_one = jnp.einsum('nfi,fh->nhi', block_inputs.astype(jnp.float32), w_one) + bias_one
        act_one = jax.nn.silu(pre_one).astype(jnp.bfloat16)
        pre_two = jnp.einsum('nhi,hk->nki', act_one.astype(jnp.float32), w_two) + bias_two
        act_two = jax.nn.silu(pre_two).astype(jnp.bfloat16)
        return jnp.einsum('nki,kl->nli', act_two.astype(jnp.float32), w_out).astype(jnp.bfloat16)

    tendency = lax.map(network, inputs)
    placed = jnp.zeros((NDOM, NB, LEV, BLK), jnp.float32).at[source, block].set(tendency.astype(jnp.float32))
    live = (jnp.arange(BLK, dtype=jnp.int32)[None, None, :] < block_count[:, :, None]).astype(jnp.float32)
    placed = placed * live[:, :, None, :]
    added = placed.transpose(2, 0, 1, 3).reshape(LEV, NCELL)
    return second_h.reshape(LEV, NCELL) + added
```

```python
import functools
import jax
import jax.numpy as jnp
from jax import lax
from jax.experimental import pallas as pl
from jax.experimental.pallas import tpu as pltpu
from jax.sharding import PartitionSpec as P

BLK = 128
LANES = 128
NDER = 4
F32 = jnp.float32
BF16 = jnp.bfloat16
VMEM = pl.BlockSpec(memory_space=pltpu.VMEM)
SMEM = pl.BlockSpec(memory_space=pltpu.SMEM)
PARAMS = pltpu.CompilerParams(vmem_limit_bytes=56 * 1024 * 1024)


def up16(n):
    return -(-n // 16) * 16


def row(ref, i):
    return ref[pl.ds(i, 1), :]


def level_mask(levels, shape):
    return lax.broadcasted_iota(jnp.int32, shape, 1) < levels


def loop(count, step, body):
    def run(i, carry):
        body(pl.multiple_of(i * step, step))
        return carry

    lax.fori_loop(0, count // step, run, 0)


def pack_rows(index_ref, rows_ref, out_ref, stage):
    count = index_ref.shape[0]

    def some(base):
        for u in range(16):
            stage[pl.ds(base + u, 1), :] = row(rows_ref, index_ref[base + u])

    loop(count, 16, some)
    out_ref[...] = stage[...].astype(out_ref.dtype)


def open_kernel(halo_ref, height_ref, coef_ref, rows_ref, out_ref, wide, stage):
    levels, cells = height_ref.shape
    wide[...] = jnp.zeros_like(wide)
    wide[0:levels, :] = height_ref[...]
    wide[levels : levels + 3, :] = coef_ref[...]
    for b in range(cells // BLK):
        cols = slice(b * BLK, (b + 1) * BLK)
        rows_ref[cols, :] = wide[:, cols].T
    pack_rows(halo_ref, rows_ref, out_ref, stage)


def edges_and_cells(levels, ec_ref, ce_ref, h_ref, v_ref, before_ref, after_ref, v_out, ext, dif, beside):
    cells, edges = h_ref.shape[0], v_ref.shape[0]
    margin = before_ref.shape[0]
    ext[0:cells, :] = h_ref[...]
    ext[cells : cells + margin, :] = before_ref[...].astype(F32)
    ext[cells + margin : cells + 2 * margin, :] = after_ref[...].astype(F32)

    def some_edges(base):
        for u in range(16):
            e = base + u
            dif[pl.ds(e, 1), :] = row(ext, ec_ref[edges + e]) - row(ext, ec_ref[e])

    loop(edges, 16, some_edges)

    def move(base):
        at = pl.ds(base, 128)
        v = v_ref[at, :]
        coef = v[:, levels : levels + 1]
        v_out[at, :] = jnp.where(level_mask(levels, v.shape), v - coef * dif[at, :], v)

    loop(edges, 128, move)

    def some_cells(base):
        for u in range(8):
            c = base + u
            for k in range(3):
                beside[k, pl.ds(c, 1), :] = row(v_out, ce_ref[k * cells + c])

    loop(cells, 8, some_cells)


def spread_of(levels, h, a0, a1, a2):
    return (
        h[:, levels : levels + 1] * a0
        + h[:, levels + 1 : levels + 2] * a1
        + h[:, levels + 2 : levels + 3] * a2
    )


def first_kernel(
    levels, ec_ref, ce_ref, halo_ref, sb_ref, h_ref, v_ref, before_ref, after_ref, tr_ref,
    h_out, v_out, pack_out, own_ref, other_ref, ext, dif, beside, stage,
):
    edges_and_cells(levels, ec_ref, ce_ref, h_ref, v_ref, before_ref, after_ref, v_out, ext, dif, beside)
    cells = h_ref.shape[0]
    pad = own_ref.shape[0] // (NDER + tr_ref.shape[0])

    def move(base):
        at = pl.ds(base, 128)
        h = h_ref[at, :]
        div = spread_of(levels, h, beside[0, at, :], beside[1, at, :], beside[2, at, :])
        h_out[at, :] = jnp.where(level_mask(levels, h.shape), h - div, h)

    loop(cells, 128, move)
    pack_rows(halo_ref, h_out, pack_out, stage)
    me = lax.axis_index("stack")
    half = sb_ref.shape[0] // 2
    third = 1.0 / 3.0
    for which, x_ref in ((me, own_ref), (1 - me, other_ref)):
        for j in range(half):
            b = jnp.maximum(sb_ref[which * half + j], 0)
            at = pl.ds(pl.multiple_of(b * BLK, BLK), BLK)
            cols = slice(j * BLK, (j + 1) * BLK)
            h, a0, a1, a2 = h_ref[at, :], beside[0, at, :], beside[1, at, :], beside[2, at, :]
            fields = (
                h_out[at, :],
                spread_of(levels, h, a0, a1, a2),
                (a0 * a0 + a1 * a1 + a2 * a2) * third,
                (a0 + a1 + a2) * third,
            )
            for q, field in enumerate(fields):
                x_ref[q * pad : (q + 1) * pad, cols] = field.T[0:pad, :].astype(BF16)
            for t in range(tr_ref.shape[0]):
                q = NDER + t
                x_ref[q * pad : (q + 1) * pad, cols] = tr_ref[t, :, at]


def second_kernel(levels, ec_ref, ce_ref, h_ref, v_ref, before_ref, after_ref, out_ref, moved, ext, dif, beside):
    edges_and_cells(levels, ec_ref, ce_ref, h_ref, v_ref, before_ref, after_ref, moved, ext, dif, beside)
    for b in range(h_ref.shape[0] // BLK):
        at = slice(b * BLK, (b + 1) * BLK)
        h = h_ref[at, :]
        div = spread_of(levels, h, beside[0, at, :], beside[1, at, :], beside[2, at, :])
        out_ref[:, at] = (h - div).T[0:levels, :]


def physics_kernel(sizes, x_own, x_other, p_own, p_other, keep_ref, send_ref):
    feats, hid, half, pad = sizes
    me = lax.axis_index("stack")
    bias_one = p_own[0:hid, feats + 1 : feats + 2].astype(F32)

    def dot(a, b):
        return jnp.dot(a, b, preferred_element_type=F32)

    def silu(v):
        return (v / (1.0 + jnp.exp(-v))).astype(BF16)

    for base in range(0, x_own.shape[1], 256):
        at = slice(base, base + 256)
        one = dot(p_own[0:hid, 0:feats], x_own[:, at]) + dot(p_other[0:hid, 0:feats], x_other[:, at])
        one = silu(one + bias_one)
        twos = []
        for p in (p_own, p_other):
            bias_two = p[0:half, feats : feats + 1].astype(F32)
            twos.append(silu(dot(p[hid : hid + half, :], one) + bias_two))
        for ref, which in ((keep_ref, me), (send_ref, 1 - me)):
            start = pl.multiple_of(hid + half + which * pad, 16)
            total = dot(p_own[pl.ds(start, pad), 0:half], twos[0])
            total += dot(p_other[pl.ds(start, pad), 0:half], twos[1])
            ref[:, at] = total.astype(BF16)


def close_kernel(sb_ref, count_ref, h_ref, keep_ref, got_ref, out_ref):
    levels = h_ref.shape[0]
    me = lax.axis_index("stack")
    half = sb_ref.shape[0] // 2
    out_ref[...] = h_ref[...]
    lane = lax.broadcasted_iota(jnp.int32, (keep_ref.shape[0], BLK), 1)
    for which, ref in ((me, keep_ref), (1 - me, got_ref)):
        for j in range(half):
            s = which * half + j
            b = jnp.maximum(sb_ref[s], 0)
            at = pl.ds(pl.multiple_of(b * BLK, BLK), BLK)
            tend = ref[:, j * BLK : (j + 1) * BLK].astype(F32)
            tend = jnp.where(lane < count_ref[s], tend, 0.0)
            out_ref[:, at] = out_ref[:, at] + tend[0:levels, :]


def body(
    height, velocity, tracers, edge_coef, cell_coef, halo_send, edge_cells, cell_edges,
    send_block, recv_slot, block_count, w_first, b_first, w_second, b_second, w_third,
):
    levels, cells = height.shape
    edges = velocity.shape[1]
    margin = halo_send.shape[1] // 2
    slots = send_block.shape[1]
    half_slots = slots // 2
    cap = slots // lax.axis_size("cells")
    nq = NDER + tracers.shape[0]
    pad = up16(levels + 3)
    feats = nq * pad
    hid, half = w_second.shape
    ring = ("cells", "role")
    size = lax.axis_size(ring)
    up = [(i, (i + 1) % size) for i in range(size)]
    down = [(j, i) for i, j in up]
    swap = [(0, 1), (1, 0)]
    halo = halo_send.reshape(-1)
    ec = edge_cells.reshape(-1)
    ce = cell_edges.reshape(-1)
    sb = send_block.reshape(-1)

    def shape(dims, dtype):
        return jax.ShapeDtypeStruct(dims, dtype)

    def exchange(packed):
        before = lax.ppermute(packed[margin:], ring, up)
        after = lax.ppermute(packed[:margin], ring, down)
        return before, after

    h_rows, packed = pl.pallas_call(
        open_kernel,
        out_shape=(shape((cells, LANES), F32), shape((2 * margin, LANES), BF16)),
        in_specs=[SMEM, VMEM, VMEM],
        out_specs=(VMEM, VMEM),
        scratch_shapes=[pltpu.VMEM((LANES, cells), F32), pltpu.VMEM((2 * margin, LANES), F32)],
        compiler_params=PARAMS,
        name="open_rows",
    )(halo, height, cell_coef)
    before, after = exchange(packed)

    one = w_first.reshape(levels, nq, hid).transpose(2, 1, 0)
    one = jnp.pad(one, ((0, 0), (0, 0), (0, pad - levels))).reshape(hid, feats)
    bias_two = jnp.pad(b_second, (0, hid - half))
    one = jnp.concatenate([one, bias_two[:, None], b_first[:, None]], axis=1)
    one = jnp.pad(one, ((0, 0), (0, hid - one.shape[1])))
    three = jnp.pad(w_third.T.reshape(2, levels, half), ((0, 0), (0, pad - levels), (0, 0)))
    three = jnp.pad(three.reshape(2 * pad, half), ((0, 0), (0, hid - half)))
    mine = jnp.concatenate([one, w_second.T, three], axis=0)
    theirs = lax.ppermute(mine, "stack", swap)

    v_rows = jnp.pad(
        jnp.concatenate([velocity, edge_coef[None]], axis=0), ((0, LANES - levels - 1), (0, 0))
    ).T
    tracers = jnp.pad(tracers, ((0, 0), (0, pad - levels), (0, 0)))

    wanted = lax.all_gather(recv_slot[0], "cells")
    slot = jnp.arange(slots, dtype=jnp.int32)
    entry = lax.axis_index("cells") * cap + slot % cap
    dest = jnp.arange(wanted.shape[0], dtype=jnp.int32)
    match = (wanted[None] == entry[:, None, None]) & (dest[None, :, None] == (slot // cap)[:, None, None])
    block = jnp.arange(cells // BLK, dtype=jnp.int32)
    counts = jnp.sum(jnp.where(sb[:, None] == block[None], block_count[0][None], 0), axis=1)
    counts = jnp.where(jnp.any(match, axis=(1, 2)), counts, 0).astype(jnp.int32)

    field_scratch = [
        pltpu.VMEM((cells + 2 * margin, LANES), F32),
        pltpu.VMEM((edges, LANES), F32),
        pltpu.VMEM((3, cells, LANES), F32),
    ]
    x_shape = shape((feats, half_slots * BLK), BF16)
    h_rows, v_rows, packed, x_own, x_send = pl.pallas_call(
        functools.partial(first_kernel, levels),
        out_shape=(
            shape((cells, LANES), F32),
            shape((edges, LANES), F32),
            shape((2 * margin, LANES), BF16),
            x_shape,
            x_shape,
        ),
        in_specs=[SMEM] * 4 + [VMEM] * 5,
        out_specs=(VMEM,) * 5,
        scratch_shapes=field_scratch + [pltpu.VMEM((2 * margin, LANES), F32)],
        compiler_params=PARAMS,
        name="first_substep",
    )(ec, ce, halo, sb, h_rows, v_rows, before, after, tracers)
    x_other = lax.ppermute(x_send, "stack", swap)
    before, after = exchange(packed)

    t_shape = shape((pad, half_slots * BLK), BF16)
    keep, send = pl.pallas_call(
        functools.partial(physics_kernel, (feats, hid, half, pad)),
        out_shape=(t_shape, t_shape),
        in_specs=[VMEM] * 4,
        out_specs=(VMEM, VMEM),
        compiler_params=PARAMS,
        cost_estimate=pl.CostEstimate(flops=2 * 10**9, bytes_accessed=4 * 10**6, transcendentals=10**6),
        name="physics",
    )(x_own, x_other, mine, theirs)
    got = lax.ppermute(send, "stack", swap)

    h_second = pl.pallas_call(
        functools.partial(second_kernel, levels),
        out_shape=shape((levels, cells), F32),
        in_specs=[SMEM] * 2 + [VMEM] * 4,
        out_specs=VMEM,
        scratch_shapes=[pltpu.VMEM((edges, LANES), F32)] + field_scratch,
        compiler_params=PARAMS,
        cost_estimate=pl.CostEstimate(flops=2 * 10**10, bytes_accessed=50 * 10**6, transcendentals=0),
        name="second_substep",
    )(ec, ce, h_rows, v_rows, before, after)

    return pl.pallas_call(
        close_kernel,
        out_shape=shape((levels, cells), F32),
        in_specs=[SMEM] * 2 + [VMEM] * 3,
        out_specs=VMEM,
        compiler_params=PARAMS,
        name="close_add",
    )(sb, counts, h_second, keep, got)


def solution(mesh):
    placed = (
        P("stack", ("groups", "cells", "role")),
        P("stack", ("groups", "cells", "role")),
        P(None, "stack", ("groups", "cells", "role")),
        P(("cells", "role")),
        P(None, ("cells", "role")),
        P(("cells", "role"), None),
        P(("cells", "role"), None, None),
        P(("cells", "role"), None, None),
        P(("cells", "role"), None),
        P(("cells", "role"), None),
        P(("cells", "role"), None),
        P("stack", None),
        P(),
        P(None, "stack"),
        P("stack"),
        P("stack", None),
    )
    return jax.shard_map(
        body,
        mesh=mesh,
        in_specs=placed,
        out_specs=P("stack", ("groups", "cells", "role")),
        check_vma=False,
    )
```

```python
import functools
import jax
import jax.numpy as jnp
from jax import lax
from jax.experimental import pallas as pl
from jax.experimental.pallas import tpu as pltpu
from jax.sharding import PartitionSpec as P

BLK = 128
LANES = 128
NDER = 4
F32 = jnp.float32
BF16 = jnp.bfloat16
VMEM = pl.BlockSpec(memory_space=pltpu.VMEM)
SMEM = pl.BlockSpec(memory_space=pltpu.SMEM)
PARAMS = pltpu.CompilerParams(vmem_limit_bytes=56 * 1024 * 1024)


def remote_params(collective_id):
    return pltpu.CompilerParams(
        vmem_limit_bytes=56 * 1024 * 1024, collective_id=collective_id, has_side_effects=True
    )


def up16(n):
    return -(-n // 16) * 16


def row(ref, i):
    return ref[pl.ds(i, 1), :]


def level_mask(levels, shape):
    return lax.broadcasted_iota(jnp.int32, shape, 1) < levels


def loop(count, step, body):
    def run(i, carry):
        body(pl.multiple_of(i * step, step))
        return carry

    lax.fori_loop(0, count // step, run, 0)


def pack_rows(index_ref, rows_ref, out_ref, stage):
    count = index_ref.shape[0]

    def some(base):
        for u in range(16):
            stage[pl.ds(base + u, 1), :] = row(rows_ref, index_ref[base + u])

    loop(count, 16, some)
    out_ref[...] = stage[...].astype(out_ref.dtype)


def remote(src, dst, sems, at, target):
    return pltpu.make_async_remote_copy(
        src_ref=src,
        dst_ref=dst,
        send_sem=sems.at[0, at],
        recv_sem=sems.at[1, at],
        device_id=target,
        device_id_type=pl.DeviceIdType.MESH,
    )


def greet(targets):
    barrier = pltpu.get_barrier_semaphore()
    for target in targets:
        pl.semaphore_signal(barrier, inc=1, device_id=target, device_id_type=pl.DeviceIdType.MESH)
    pl.semaphore_wait(barrier, len(targets))


def around_ring(n_cells, n_role):
    size = n_cells * n_role
    me = lax.axis_index("cells") * n_role + lax.axis_index("role")
    found = []
    for step in (1, size - 1):
        there = lax.rem(me + step, size)
        found.append({"cells": lax.div(there, n_role), "role": lax.rem(there, n_role)})
    return found


def halo_copies(packed, before, after, sems, ring):
    margin = packed.shape[0] // 2
    return [
        remote(packed.at[pl.ds(margin, margin)], before, sems, 0, ring[0]),
        remote(packed.at[pl.ds(0, margin)], after, sems, 1, ring[1]),
    ]


def to_rows(field_ref, extra_ref, rows_ref, wide):
    levels, count = field_ref.shape
    extra = extra_ref.shape[0]
    wide[0:levels, 0:count] = field_ref[...]
    wide[levels : levels + extra, 0:count] = extra_ref[...]
    for b in range(count // BLK):
        cols = slice(b * BLK, (b + 1) * BLK)
        rows_ref[cols, :] = wide[:, cols].T


def open_kernel(
    mesh_size, halo_ref, height_ref, coef_ref, velocity_ref, edge_ref, recv_ref,
    rows_ref, v_ref, before_ref, after_ref, table_ref, wide, stage, packed, sems,
):
    n_cells, n_role = mesh_size
    ring = around_ring(n_cells, n_role)
    me = lax.axis_index("cells")
    peers = [{"cells": lax.rem(me + step, n_cells)} for step in range(1, n_cells)]
    greet(ring + peers)
    copies = [
        remote(recv_ref, table_ref.at[me], sems, 2 + i, peer) for i, peer in enumerate(peers)
    ]
    for copy in copies:
        copy.start()
    table_ref[me] = recv_ref[...]
    wide[...] = jnp.zeros_like(wide)
    to_rows(height_ref, coef_ref, rows_ref, wide)
    pack_rows(halo_ref, rows_ref, packed, stage)
    halos = halo_copies(packed, before_ref, after_ref, sems, ring)
    for copy in halos:
        copy.start()
    to_rows(velocity_ref, edge_ref, v_ref, wide)
    for copy in copies + halos:
        copy.wait()


def edges_and_cells(levels, ec_ref, ce_ref, h_ref, v_ref, before_ref, after_ref, v_out, ext, dif, beside):
    cells, edges = h_ref.shape[0], v_ref.shape[0]
    margin = before_ref.shape[0]
    ext[0:cells, :] = h_ref[...]
    ext[cells : cells + margin, :] = before_ref[...].astype(F32)
    ext[cells + margin : cells + 2 * margin, :] = after_ref[...].astype(F32)

    def some_edges(base):
        found = []
        for u in range(32):
            e = base + u
            found.append(row(ext, ec_ref[edges + e]) - row(ext, ec_ref[e]))
        for u in range(32):
            dif[pl.ds(base + u, 1), :] = found[u]

    loop(edges, 32, some_edges)

    def move(base):
        at = pl.ds(base, 128)
        v = v_ref[at, :]
        coef = v[:, levels : levels + 1]
        v_out[at, :] = jnp.where(level_mask(levels, v.shape), v - coef * dif[at, :], v)

    loop(edges, 128, move)

    def some_cells(base):
        found = []
        for u in range(16):
            for k in range(3):
                found.append((u, k, row(v_out, ce_ref[k * cells + base + u])))
        for u, k, value in found:
            beside[k, pl.ds(base + u, 1), :] = value

    loop(cells, 16, some_cells)


def spread_of(levels, h, a0, a1, a2):
    return (
        h[:, levels : levels + 1] * a0
        + h[:, levels + 1 : levels + 2] * a1
        + h[:, levels + 2 : levels + 3] * a2
    )


def first_kernel(
    levels, ec_ref, ce_ref, halo_ref, sb_ref, h_ref, v_ref, before_ref, after_ref, tr_ref,
    h_out, v_out, pack_out, own_ref, other_ref, ext, dif, beside, stage,
):
    edges_and_cells(levels, ec_ref, ce_ref, h_ref, v_ref, before_ref, after_ref, v_out, ext, dif, beside)
    cells = h_ref.shape[0]
    pad = own_ref.shape[0] // (NDER + tr_ref.shape[0])

    def move(base):
        at = pl.ds(base, 128)
        h = h_ref[at, :]
        div = spread_of(levels, h, beside[0, at, :], beside[1, at, :], beside[2, at, :])
        h_out[at, :] = jnp.where(level_mask(levels, h.shape), h - div, h)

    loop(cells, 128, move)
    pack_rows(halo_ref, h_out, pack_out, stage)
    me = lax.axis_index("stack")
    half = sb_ref.shape[0] // 2
    third = 1.0 / 3.0
    for x_ref in (own_ref, other_ref):
        for t in range(tr_ref.shape[0]):
            end = (NDER + t + 1) * pad
            x_ref[end - 16 : end, :] = jnp.zeros((16, x_ref.shape[1]), BF16)
    for which, x_ref in ((me, own_ref), (1 - me, other_ref)):
        for j in range(half):
            b = jnp.maximum(sb_ref[which * half + j], 0)
            at = pl.ds(pl.multiple_of(b * BLK, BLK), BLK)
            cols = slice(j * BLK, (j + 1) * BLK)
            h, a0, a1, a2 = h_ref[at, :], beside[0, at, :], beside[1, at, :], beside[2, at, :]
            fields = (
                h_out[at, :],
                spread_of(levels, h, a0, a1, a2),
                (a0 * a0 + a1 * a1 + a2 * a2) * third,
                (a0 + a1 + a2) * third,
            )
            for q, field in enumerate(fields):
                x_ref[q * pad : (q + 1) * pad, cols] = field.T[0:pad, :].astype(BF16)
            for t in range(tr_ref.shape[0]):
                q = NDER + t
                x_ref[q * pad : q * pad + levels, cols] = tr_ref[t, :, at]


def second_kernel(levels, ec_ref, ce_ref, h_ref, v_ref, before_ref, after_ref, out_ref, moved, ext, dif, beside):
    edges_and_cells(levels, ec_ref, ce_ref, h_ref, v_ref, before_ref, after_ref, moved, ext, dif, beside)
    for b in range(h_ref.shape[0] // BLK):
        at = slice(b * BLK, (b + 1) * BLK)
        h = h_ref[at, :]
        div = spread_of(levels, h, beside[0, at, :], beside[1, at, :], beside[2, at, :])
        out_ref[:, at] = (h - div).T[0:levels, :]


def physics_kernel(
    sizes, x_own, x_mine, packed, p_own, p_other,
    keep_ref, send_ref, before_ref, after_ref, x_other, sems,
):
    feats, hid, half, pad, n_cells, n_role = sizes
    me = lax.axis_index("stack")
    ring = around_ring(n_cells, n_role)
    twin = {"stack": 1 - me}
    greet(ring + [twin])
    halos = halo_copies(packed, before_ref, after_ref, sems, ring)
    swap = remote(x_mine, x_other, sems, 2, twin)
    for copy in [swap] + halos:
        copy.start()
    swap.wait()
    bias_one = p_own[0:hid, feats + 1 : feats + 2].astype(F32)

    def dot(a, b):
        return jnp.dot(a, b, preferred_element_type=F32)

    def silu(v):
        return (v / (1.0 + jnp.exp(-v))).astype(BF16)

    for base in range(0, x_own.shape[1], 256):
        at = slice(base, base + 256)
        one = dot(p_own[0:hid, 0:feats], x_own[:, at]) + dot(p_other[0:hid, 0:feats], x_other[:, at])
        one = silu(one + bias_one)
        twos = []
        for p in (p_own, p_other):
            bias_two = p[0:half, feats : feats + 1].astype(F32)
            twos.append(silu(dot(p[hid : hid + half, :], one) + bias_two))
        for ref, which in ((keep_ref, me), (send_ref, 1 - me)):
            start = pl.multiple_of(hid + half + which * pad, 16)
            total = dot(p_own[pl.ds(start, pad), 0:half], twos[0])
            total += dot(p_other[pl.ds(start, pad), 0:half], twos[1])
            ref[:, at] = total.astype(BF16)
    for copy in halos:
        copy.wait()


def close_kernel(sb_ref, count_ref, h_ref, keep_ref, got_ref, out_ref):
    levels = h_ref.shape[0]
    me = lax.axis_index("stack")
    half = sb_ref.shape[0] // 2
    out_ref[...] = h_ref[...]
    lane = lax.broadcasted_iota(jnp.int32, (keep_ref.shape[0], BLK), 1)
    for which, ref in ((me, keep_ref), (1 - me, got_ref)):
        for j in range(half):
            s = which * half + j
            b = jnp.maximum(sb_ref[s], 0)
            at = pl.ds(pl.multiple_of(b * BLK, BLK), BLK)
            tend = ref[:, j * BLK : (j + 1) * BLK].astype(F32)
            tend = jnp.where(lane < count_ref[s], tend, 0.0)
            out_ref[:, at] = out_ref[:, at] + tend[0:levels, :]


def body(
    height, velocity, tracers, edge_coef, cell_coef, halo_send, edge_cells, cell_edges,
    send_block, recv_slot, block_count, w_first, b_first, w_second, b_second, w_third,
):
    n_cells, n_role = lax.axis_size("cells"), lax.axis_size("role")
    levels, cells = height.shape
    edges = velocity.shape[1]
    margin = halo_send.shape[1] // 2
    slots = send_block.shape[1]
    half_slots = slots // 2
    cap = slots // n_cells
    nq = NDER + tracers.shape[0]
    pad = up16(levels + 3)
    feats = nq * pad
    hid, half = w_second.shape
    swap = [(0, 1), (1, 0)]
    halo = halo_send.reshape(-1)
    ec = edge_cells.reshape(-1)
    ce = cell_edges.reshape(-1)
    sb = send_block.reshape(-1)

    def shape(dims, dtype):
        return jax.ShapeDtypeStruct(dims, dtype)

    halo_shape = shape((margin, LANES), BF16)
    recv = jnp.pad(recv_slot, ((0, 0), (0, LANES - recv_slot.shape[1])), constant_values=-1)
    h_rows, v_rows, before, after, wanted = pl.pallas_call(
        functools.partial(open_kernel, (n_cells, n_role)),
        out_shape=(
            shape((cells, LANES), F32),
            shape((edges, LANES), F32),
            halo_shape,
            halo_shape,
            shape((n_cells, 1, LANES), jnp.int32),
        ),
        in_specs=[SMEM] + [VMEM] * 5,
        out_specs=(VMEM,) * 5,
        scratch_shapes=[
            pltpu.VMEM((LANES, max(cells, edges)), F32),
            pltpu.VMEM((2 * margin, LANES), F32),
            pltpu.VMEM((2 * margin, LANES), BF16),
            pltpu.SemaphoreType.DMA((2, n_cells + 1)),
        ],
        compiler_params=remote_params(0),
        name="open_rows",
    )(halo, height, cell_coef, velocity, edge_coef[None], recv)
    wanted = wanted.reshape(n_cells, LANES)

    one = w_first.reshape(levels, nq, hid).transpose(2, 1, 0)
    one = jnp.pad(one, ((0, 0), (0, 0), (0, pad - levels))).reshape(hid, feats)
    bias_two = jnp.pad(b_second, (0, hid - half))
    one = jnp.concatenate([one, bias_two[:, None], b_first[:, None]], axis=1)
    one = jnp.pad(one, ((0, 0), (0, hid - one.shape[1])))
    three = jnp.pad(w_third.T.reshape(2, levels, half), ((0, 0), (0, pad - levels), (0, 0)))
    three = jnp.pad(three.reshape(2 * pad, half), ((0, 0), (0, hid - half)))
    mine = jnp.concatenate([one, w_second.T, three], axis=0)
    theirs = lax.ppermute(mine, "stack", swap)

    slot = jnp.arange(slots, dtype=jnp.int32)
    entry = lax.axis_index("cells") * cap + slot % cap
    dest = jnp.arange(wanted.shape[0], dtype=jnp.int32)
    match = (wanted[None] == entry[:, None, None]) & (dest[None, :, None] == (slot // cap)[:, None, None])
    block = jnp.arange(cells // BLK, dtype=jnp.int32)
    counts = jnp.sum(jnp.where(sb[:, None] == block[None], block_count[0][None], 0), axis=1)
    counts = jnp.where(jnp.any(match, axis=(1, 2)), counts, 0).astype(jnp.int32)

    field_scratch = [
        pltpu.VMEM((cells + 2 * margin, LANES), F32),
        pltpu.VMEM((edges, LANES), F32),
        pltpu.VMEM((3, cells, LANES), F32),
    ]
    x_shape = shape((feats, half_slots * BLK), BF16)
    h_rows, v_rows, packed, x_own, x_send = pl.pallas_call(
        functools.partial(first_kernel, levels),
        out_shape=(
            shape((cells, LANES), F32),
            shape((edges, LANES), F32),
            shape((2 * margin, LANES), BF16),
            x_shape,
            x_shape,
        ),
        in_specs=[SMEM] * 4 + [VMEM] * 5,
        out_specs=(VMEM,) * 5,
        scratch_shapes=field_scratch + [pltpu.VMEM((2 * margin, LANES), F32)],
        compiler_params=PARAMS,
        name="first_substep",
    )(ec, ce, halo, sb, h_rows, v_rows, before, after, tracers)

    t_shape = shape((pad, half_slots * BLK), BF16)
    keep, send, before, after = pl.pallas_call(
        functools.partial(physics_kernel, (feats, hid, half, pad, n_cells, n_role)),
        out_shape=(t_shape, t_shape, halo_shape, halo_shape),
        in_specs=[VMEM] * 5,
        out_specs=(VMEM,) * 4,
        scratch_shapes=[pltpu.VMEM(x_shape.shape, BF16), pltpu.SemaphoreType.DMA((2, 3))],
        compiler_params=remote_params(1),
        cost_estimate=pl.CostEstimate(flops=2 * 10**9, bytes_accessed=4 * 10**6, transcendentals=10**6),
        name="physics",
    )(x_own, x_send, packed, mine, theirs)
    got = lax.ppermute(send, "stack", swap)

    h_second = pl.pallas_call(
        functools.partial(second_kernel, levels),
        out_shape=shape((levels, cells), F32),
        in_specs=[SMEM] * 2 + [VMEM] * 4,
        out_specs=VMEM,
        scratch_shapes=[pltpu.VMEM((edges, LANES), F32)] + field_scratch,
        compiler_params=PARAMS,
        cost_estimate=pl.CostEstimate(flops=2 * 10**10, bytes_accessed=50 * 10**6, transcendentals=0),
        name="second_substep",
    )(ec, ce, h_rows, v_rows, before, after)

    return pl.pallas_call(
        close_kernel,
        out_shape=shape((levels, cells), F32),
        in_specs=[SMEM] * 2 + [VMEM] * 3,
        out_specs=VMEM,
        compiler_params=PARAMS,
        name="close_add",
    )(sb, counts, h_second, keep, got)


def solution(mesh):
    placed = (
        P("stack", ("groups", "cells", "role")),
        P("stack", ("groups", "cells", "role")),
        P(None, "stack", ("groups", "cells", "role")),
        P(("cells", "role")),
        P(None, ("cells", "role")),
        P(("cells", "role"), None),
        P(("cells", "role"), None, None),
        P(("cells", "role"), None, None),
        P(("cells", "role"), None),
        P(("cells", "role"), None),
        P(("cells", "role"), None),
        P("stack", None),
        P(),
        P(None, "stack"),
        P("stack"),
        P("stack", None),
    )
    return jax.shard_map(
        body,
        mesh=mesh,
        in_specs=placed,
        out_specs=P("stack", ("groups", "cells", "role")),
        check_vma=False,
    )
```

```python
import functools
import jax
import jax.numpy as jnp
from jax import lax
from jax.experimental import pallas as pl
from jax.experimental.pallas import tpu as pltpu
from jax.sharding import PartitionSpec as P

BLK = 128
LANES = 128
NDER = 4
F32 = jnp.float32
BF16 = jnp.bfloat16
VMEM = pl.BlockSpec(memory_space=pltpu.VMEM)
SMEM = pl.BlockSpec(memory_space=pltpu.SMEM)
PARAMS = pltpu.CompilerParams(vmem_limit_bytes=56 * 1024 * 1024)


def remote_params(collective_id):
    return pltpu.CompilerParams(
        vmem_limit_bytes=56 * 1024 * 1024, collective_id=collective_id, has_side_effects=True
    )


def up16(n):
    return -(-n // 16) * 16


def row(ref, i):
    return ref[pl.ds(i, 1), :]


def level_mask(levels, shape):
    return lax.broadcasted_iota(jnp.int32, shape, 1) < levels


def loop(count, step, body):
    def run(i, carry):
        body(pl.multiple_of(i * step, step))
        return carry

    lax.fori_loop(0, count // step, run, 0)


def pack_rows(index_ref, rows_ref, out_ref, stage):
    count = index_ref.shape[0]

    def some(base):
        for u in range(16):
            stage[pl.ds(base + u, 1), :] = row(rows_ref, index_ref[base + u])

    loop(count, 16, some)
    out_ref[...] = stage[...].astype(out_ref.dtype)


def remote(src, dst, sems, at, target):
    return pltpu.make_async_remote_copy(
        src_ref=src,
        dst_ref=dst,
        send_sem=sems.at[0, at],
        recv_sem=sems.at[1, at],
        device_id=target,
        device_id_type=pl.DeviceIdType.MESH,
    )


def greet(targets):
    barrier = pltpu.get_barrier_semaphore()
    for target in targets:
        pl.semaphore_signal(barrier, inc=1, device_id=target, device_id_type=pl.DeviceIdType.MESH)
    pl.semaphore_wait(barrier, len(targets))


def around_ring(n_cells, n_role):
    size = n_cells * n_role
    me = lax.axis_index("cells") * n_role + lax.axis_index("role")
    found = []
    for step in (1, size - 1):
        there = lax.rem(me + step, size)
        found.append({"cells": lax.div(there, n_role), "role": lax.rem(there, n_role)})
    return found


def halo_copies(packed, before, after, sems, ring):
    margin = packed.shape[0] // 2
    return [
        remote(packed.at[pl.ds(margin, margin)], before, sems, 0, ring[0]),
        remote(packed.at[pl.ds(0, margin)], after, sems, 1, ring[1]),
    ]


def to_rows(field_ref, extra_ref, rows_ref, wide):
    levels, count = field_ref.shape
    extra = extra_ref[...].reshape(-1, count)
    wide[0:levels, 0:count] = field_ref[...]
    wide[levels : levels + extra.shape[0], 0:count] = extra
    for b in range(count // BLK):
        cols = slice(b * BLK, (b + 1) * BLK)
        rows_ref[cols, :] = wide[:, cols].T


def open_kernel(
    mesh_size, halo_ref, height_ref, coef_ref, velocity_ref, edge_ref, recv_ref,
    rows_ref, v_ref, before_ref, after_ref, table_ref, wide, stage, packed, sems,
):
    n_cells, n_role = mesh_size
    ring = around_ring(n_cells, n_role)
    me = lax.axis_index("cells")
    peers = [{"cells": lax.rem(me + step, n_cells)} for step in range(1, n_cells)]
    greet(ring + peers)
    copies = [
        remote(recv_ref, table_ref.at[me], sems, 2 + i, peer) for i, peer in enumerate(peers)
    ]
    for copy in copies:
        copy.start()
    table_ref[me] = recv_ref[...]
    wide[...] = jnp.zeros_like(wide)
    to_rows(height_ref, coef_ref, rows_ref, wide)
    pack_rows(halo_ref, rows_ref, packed, stage)
    halos = halo_copies(packed, before_ref, after_ref, sems, ring)
    for copy in halos:
        copy.start()
    to_rows(velocity_ref, edge_ref, v_ref, wide)
    for copy in copies + halos:
        copy.wait()


def edges_and_cells(levels, ec_ref, ce_ref, h_ref, v_ref, before_ref, after_ref, v_out, ext, dif, beside):
    cells, edges = h_ref.shape[0], v_ref.shape[0]
    margin = before_ref.shape[0]
    ext[0:cells, :] = h_ref[...]
    ext[cells : cells + margin, :] = before_ref[...].astype(F32)
    ext[cells + margin : cells + 2 * margin, :] = after_ref[...].astype(F32)

    def some_edges(base):
        found = []
        for u in range(32):
            e = base + u
            found.append(row(ext, ec_ref[edges + e]) - row(ext, ec_ref[e]))
        for u in range(32):
            dif[pl.ds(base + u, 1), :] = found[u]

    loop(edges, 32, some_edges)

    def move(base):
        at = pl.ds(base, 128)
        v = v_ref[at, :]
        coef = v[:, levels : levels + 1]
        v_out[at, :] = jnp.where(level_mask(levels, v.shape), v - coef * dif[at, :], v)

    loop(edges, 128, move)

    def some_cells(base):
        found = []
        for u in range(16):
            for k in range(3):
                found.append((u, k, row(v_out, ce_ref[k * cells + base + u])))
        for u, k, value in found:
            beside[k, pl.ds(base + u, 1), :] = value

    loop(cells, 16, some_cells)


def spread_of(levels, h, a0, a1, a2):
    return (
        h[:, levels : levels + 1] * a0
        + h[:, levels + 1 : levels + 2] * a1
        + h[:, levels + 2 : levels + 3] * a2
    )


def first_kernel(
    levels, ec_ref, ce_ref, halo_ref, sb_ref, h_ref, v_ref, before_ref, after_ref, tr_ref,
    h_out, v_out, pack_out, own_ref, other_ref, ext, dif, beside, stage,
):
    edges_and_cells(levels, ec_ref, ce_ref, h_ref, v_ref, before_ref, after_ref, v_out, ext, dif, beside)
    cells = h_ref.shape[0]
    pad = own_ref.shape[0] // (NDER + tr_ref.shape[0])

    def move(base):
        at = pl.ds(base, 128)
        h = h_ref[at, :]
        div = spread_of(levels, h, beside[0, at, :], beside[1, at, :], beside[2, at, :])
        h_out[at, :] = jnp.where(level_mask(levels, h.shape), h - div, h)

    loop(cells, 128, move)
    pack_rows(halo_ref, h_out, pack_out, stage)
    me = lax.axis_index("stack")
    half = sb_ref.shape[0] // 2
    third = 1.0 / 3.0
    for x_ref in (own_ref, other_ref):
        for t in range(tr_ref.shape[0]):
            end = (NDER + t + 1) * pad
            x_ref[end - 16 : end, :] = jnp.zeros((16, x_ref.shape[1]), BF16)
    for which, x_ref in ((me, own_ref), (1 - me, other_ref)):
        for j in range(half):
            b = jnp.maximum(sb_ref[which * half + j], 0)
            at = pl.ds(pl.multiple_of(b * BLK, BLK), BLK)
            cols = slice(j * BLK, (j + 1) * BLK)
            h, a0, a1, a2 = h_ref[at, :], beside[0, at, :], beside[1, at, :], beside[2, at, :]
            fields = (
                h_out[at, :],
                spread_of(levels, h, a0, a1, a2),
                (a0 * a0 + a1 * a1 + a2 * a2) * third,
                (a0 + a1 + a2) * third,
            )
            for q, field in enumerate(fields):
                x_ref[q * pad : (q + 1) * pad, cols] = field.T[0:pad, :].astype(BF16)
            for t in range(tr_ref.shape[0]):
                q = NDER + t
                x_ref[q * pad : q * pad + levels, cols] = tr_ref[t, :, at]


def second_kernel(levels, ec_ref, ce_ref, h_ref, v_ref, before_ref, after_ref, out_ref, moved, ext, dif, beside):
    edges_and_cells(levels, ec_ref, ce_ref, h_ref, v_ref, before_ref, after_ref, moved, ext, dif, beside)
    for b in range(h_ref.shape[0] // BLK):
        at = slice(b * BLK, (b + 1) * BLK)
        h = h_ref[at, :]
        div = spread_of(levels, h, beside[0, at, :], beside[1, at, :], beside[2, at, :])
        out_ref[:, at] = (h - div).T[0:levels, :]


def by_quantity(w_ref, nq, pad):
    rows, hid = w_ref.shape
    levels = rows // nq
    level = lax.broadcasted_iota(jnp.int32, (pad, rows), 0)
    entry = lax.broadcasted_iota(jnp.int32, (pad, rows), 1)
    parts = []
    for q in range(nq):
        chosen = (entry == level * nq + q) & (level < levels)
        chosen = jnp.where(chosen, 1.0, 0.0).astype(BF16)
        parts.append(jnp.dot(chosen, w_ref[...], preferred_element_type=F32).T)
    return jnp.concatenate(parts, axis=1).astype(BF16)


def physics_kernel(
    sizes, x_own, x_mine, packed, bias_one, *refs
):
    weights, refs = refs[:8], refs[8:]
    keep_ref, send_ref, before_ref, after_ref, x_other, first, sems = refs
    nq, pad, n_cells, n_role = sizes
    me = lax.axis_index("stack")
    ring = around_ring(n_cells, n_role)
    twin = {"stack": 1 - me}
    greet(ring + [twin])
    halos = halo_copies(packed, before_ref, after_ref, sems, ring)
    swap = remote(x_mine, x_other, sems, 2, twin)
    for copy in [swap] + halos:
        copy.start()
    ours, theirs = weights[:4], weights[4:]
    first[0] = by_quantity(ours[0], nq, pad)
    first[1] = by_quantity(theirs[0], nq, pad)
    swap.wait()

    def dot(a, b):
        return jnp.dot(a, b, preferred_element_type=F32)

    def across(a, b):
        return lax.dot_general(a, b, (((0,), (0,)), ((), ())), preferred_element_type=F32)

    def silu(v):
        return (v / (1.0 + jnp.exp(-v))).astype(BF16)

    chunk = 256
    levels = ours[2].shape[1] // 2
    ones = jnp.ones((1, chunk), BF16)
    for base in range(0, x_own.shape[1], chunk):
        at = slice(base, base + chunk)
        one = dot(first[0], x_own[:, at]) + dot(first[1], x_other[:, at])
        one = silu(one + across(bias_one[...], ones))
        total = None
        for _, second, third, bias in (ours, theirs):
            two = silu(across(second[...], one) + across(bias[...], ones))
            term = across(third[...], two)
            total = term if total is None else total + term
        low, high = total[0:levels], total[levels : 2 * levels]
        keep_ref[:, at] = jnp.where(me == 0, low, high).astype(BF16).astype(F32)
        send_ref[0:levels, at] = jnp.where(me == 0, high, low).astype(BF16)
    for copy in halos:
        copy.wait()


def close_kernel(sb_ref, count_ref, h_ref, keep_ref, got_ref, out_ref):
    levels = h_ref.shape[0]
    me = lax.axis_index("stack")
    half = sb_ref.shape[0] // 2
    out_ref[...] = h_ref[...]
    lane = lax.broadcasted_iota(jnp.int32, (levels, BLK), 1)
    for which, ref in ((me, keep_ref), (1 - me, got_ref)):
        for j in range(half):
            s = which * half + j
            b = jnp.maximum(sb_ref[s], 0)
            at = pl.ds(pl.multiple_of(b * BLK, BLK), BLK)
            tend = ref[:, j * BLK : (j + 1) * BLK].astype(F32)[0:levels, :]
            tend = jnp.where(lane < count_ref[s], tend, 0.0)
            out_ref[:, at] = out_ref[:, at] + tend


def body(
    height, velocity, tracers, edge_coef, cell_coef, halo_send, edge_cells, cell_edges,
    send_block, recv_slot, block_count, w_first, b_first, w_second, b_second, w_third,
):
    n_cells, n_role = lax.axis_size("cells"), lax.axis_size("role")
    levels, cells = height.shape
    edges = velocity.shape[1]
    margin = halo_send.shape[1] // 2
    slots = send_block.shape[1]
    half_slots = slots // 2
    cap = slots // n_cells
    nq = NDER + tracers.shape[0]
    pad = up16(levels + 3)
    feats = nq * pad
    swap = [(0, 1), (1, 0)]
    halo = halo_send.reshape(-1)
    ec = edge_cells.reshape(-1)
    ce = cell_edges.reshape(-1)
    sb = send_block.reshape(-1)

    def shape(dims, dtype):
        return jax.ShapeDtypeStruct(dims, dtype)

    ours = (w_first, w_second, w_third, b_second[None])
    theirs = tuple(lax.ppermute(array, "stack", swap) for array in ours)
    halo_shape = shape((margin, LANES), BF16)
    recv = jnp.pad(recv_slot, ((0, 0), (0, LANES - recv_slot.shape[1])), constant_values=-1)
    h_rows, v_rows, before, after, wanted = pl.pallas_call(
        functools.partial(open_kernel, (n_cells, n_role)),
        out_shape=(
            shape((cells, LANES), F32),
            shape((edges, LANES), F32),
            halo_shape,
            halo_shape,
            shape((n_cells, 1, LANES), jnp.int32),
        ),
        in_specs=[SMEM] + [VMEM] * 5,
        out_specs=(VMEM,) * 5,
        scratch_shapes=[
            pltpu.VMEM((LANES, max(cells, edges)), F32),
            pltpu.VMEM((2 * margin, LANES), F32),
            pltpu.VMEM((2 * margin, LANES), BF16),
            pltpu.SemaphoreType.DMA((2, n_cells + 1)),
        ],
        compiler_params=remote_params(0),
        name="open_rows",
    )(halo, height, cell_coef, velocity, edge_coef, recv)
    wanted = wanted.reshape(n_cells, LANES)

    slot = jnp.arange(slots, dtype=jnp.int32)
    entry = lax.axis_index("cells") * cap + slot % cap
    dest = jnp.arange(wanted.shape[0], dtype=jnp.int32)
    match = (wanted[None] == entry[:, None, None]) & (dest[None, :, None] == (slot // cap)[:, None, None])
    block = jnp.arange(cells // BLK, dtype=jnp.int32)
    counts = jnp.sum(jnp.where(sb[:, None] == block[None], block_count[0][None], 0), axis=1)
    counts = jnp.where(jnp.any(match, axis=(1, 2)), counts, 0).astype(jnp.int32)

    field_scratch = [
        pltpu.VMEM((cells + 2 * margin, LANES), F32),
        pltpu.VMEM((edges, LANES), F32),
        pltpu.VMEM((3, cells, LANES), F32),
    ]
    x_shape = shape((feats, half_slots * BLK), BF16)
    h_rows, v_rows, packed, x_own, x_send = pl.pallas_call(
        functools.partial(first_kernel, levels),
        out_shape=(
            shape((cells, LANES), F32),
            shape((edges, LANES), F32),
            shape((2 * margin, LANES), BF16),
            x_shape,
            x_shape,
        ),
        in_specs=[SMEM] * 4 + [VMEM] * 5,
        out_specs=(VMEM,) * 5,
        scratch_shapes=field_scratch + [pltpu.VMEM((2 * margin, LANES), F32)],
        compiler_params=PARAMS,
        name="first_substep",
    )(ec, ce, halo, sb, h_rows, v_rows, before, after, tracers)

    width = half_slots * BLK
    keep, send, before, after = pl.pallas_call(
        functools.partial(physics_kernel, (nq, pad, n_cells, n_role)),
        out_shape=(shape((levels, width), F32), shape((pad, width), BF16), halo_shape, halo_shape),
        in_specs=[VMEM] * 12,
        out_specs=(VMEM,) * 4,
        scratch_shapes=[
            pltpu.VMEM(x_shape.shape, BF16),
            pltpu.VMEM((2, w_first.shape[1], feats), BF16),
            pltpu.SemaphoreType.DMA((2, 3)),
        ],
        compiler_params=remote_params(1),
        cost_estimate=pl.CostEstimate(flops=2 * 10**9, bytes_accessed=4 * 10**6, transcendentals=10**6),
        name="physics",
    )(x_own, x_send, packed, b_first[None], *ours, *theirs)
    got = lax.ppermute(send, "stack", swap)

    h_second = pl.pallas_call(
        functools.partial(second_kernel, levels),
        out_shape=shape((levels, cells), F32),
        in_specs=[SMEM] * 2 + [VMEM] * 4,
        out_specs=VMEM,
        scratch_shapes=[pltpu.VMEM((edges, LANES), F32)] + field_scratch,
        compiler_params=PARAMS,
        cost_estimate=pl.CostEstimate(flops=2 * 10**10, bytes_accessed=50 * 10**6, transcendentals=0),
        name="second_substep",
    )(ec, ce, h_rows, v_rows, before, after)

    return pl.pallas_call(
        close_kernel,
        out_shape=shape((levels, cells), F32),
        in_specs=[SMEM] * 2 + [VMEM] * 3,
        out_specs=VMEM,
        compiler_params=PARAMS,
        name="close_add",
    )(sb, counts, h_second, keep, got)


def solution(mesh):
    placed = (
        P("stack", ("groups", "cells", "role")),
        P("stack", ("groups", "cells", "role")),
        P(None, "stack", ("groups", "cells", "role")),
        P(("cells", "role")),
        P(None, ("cells", "role")),
        P(("cells", "role"), None),
        P(("cells", "role"), None, None),
        P(("cells", "role"), None, None),
        P(("cells", "role"), None),
        P(("cells", "role"), None),
        P(("cells", "role"), None),
        P("stack", None),
        P(),
        P(None, "stack"),
        P("stack"),
        P("stack", None),
    )
    return jax.shard_map(
        body,
        mesh=mesh,
        in_specs=placed,
        out_specs=P("stack", ("groups", "cells", "role")),
        check_vma=False,
    )
```

```python
import functools
import jax
import jax.numpy as jnp
from jax import lax
from jax.experimental import pallas as pl
from jax.experimental.pallas import tpu as pltpu
from jax.sharding import PartitionSpec as P

BLK = 128
LANES = 128
NDER = 4
F32 = jnp.float32
BF16 = jnp.bfloat16
VMEM = pl.BlockSpec(memory_space=pltpu.VMEM)
SMEM = pl.BlockSpec(memory_space=pltpu.SMEM)
PARAMS = pltpu.CompilerParams(vmem_limit_bytes=56 * 1024 * 1024)


def remote_params(collective_id):
    return pltpu.CompilerParams(
        vmem_limit_bytes=56 * 1024 * 1024, collective_id=collective_id, has_side_effects=True
    )


def up16(n):
    return -(-n // 16) * 16


def row(ref, i):
    return ref[pl.ds(i, 1), :]


def level_mask(levels, shape):
    return lax.broadcasted_iota(jnp.int32, shape, 1) < levels


def loop(count, step, body):
    def run(i, carry):
        body(pl.multiple_of(i * step, step))
        return carry

    lax.fori_loop(0, count // step, run, 0)


def pack_rows(index_ref, rows_ref, out_ref, stage):
    count = index_ref.shape[0]

    def some(base):
        for u in range(16):
            stage[pl.ds(base + u, 1), :] = row(rows_ref, index_ref[base + u])

    loop(count, 16, some)
    out_ref[...] = stage[...].astype(out_ref.dtype)


def remote(src, dst, sems, at, target):
    return pltpu.make_async_remote_copy(
        src_ref=src,
        dst_ref=dst,
        send_sem=sems.at[0, at],
        recv_sem=sems.at[1, at],
        device_id=target,
        device_id_type=pl.DeviceIdType.MESH,
    )


def greet(targets):
    barrier = pltpu.get_barrier_semaphore()
    for target in targets:
        pl.semaphore_signal(barrier, inc=1, device_id=target, device_id_type=pl.DeviceIdType.MESH)
    pl.semaphore_wait(barrier, len(targets))


def around_ring(n_cells, n_role):
    size = n_cells * n_role
    me = lax.axis_index("cells") * n_role + lax.axis_index("role")
    found = []
    for step in (1, size - 1):
        there = lax.rem(me + step, size)
        found.append({"cells": lax.div(there, n_role), "role": lax.rem(there, n_role)})
    return found


def halo_copies(packed, before, after, sems, ring):
    margin = packed.shape[0] // 2
    return [
        remote(packed.at[pl.ds(margin, margin)], before, sems, 0, ring[0]),
        remote(packed.at[pl.ds(0, margin)], after, sems, 1, ring[1]),
    ]


def to_rows(field_ref, extra_ref, rows_ref, wide):
    levels, count = field_ref.shape
    extra = extra_ref[...].reshape(-1, count)
    wide[0:levels, 0:count] = field_ref[...]
    wide[levels : levels + extra.shape[0], 0:count] = extra
    for b in range(count // BLK):
        cols = slice(b * BLK, (b + 1) * BLK)
        rows_ref[cols, :] = wide[:, cols].T


def open_kernel(
    mesh_size, halo_ref, height_ref, coef_ref, velocity_ref, edge_ref, recv_ref,
    rows_ref, v_ref, before_ref, after_ref, table_ref, wide, stage, packed, sems,
):
    n_cells, n_role = mesh_size
    ring = around_ring(n_cells, n_role)
    me = lax.axis_index("cells")
    peers = [{"cells": lax.rem(me + step, n_cells)} for step in range(1, n_cells)]
    greet(ring + peers)
    copies = [
        remote(recv_ref, table_ref.at[me], sems, 2 + i, peer) for i, peer in enumerate(peers)
    ]
    for copy in copies:
        copy.start()
    table_ref[me] = recv_ref[...]
    wide[...] = jnp.zeros_like(wide)
    to_rows(height_ref, coef_ref, rows_ref, wide)
    pack_rows(halo_ref, rows_ref, packed, stage)
    halos = halo_copies(packed, before_ref, after_ref, sems, ring)
    for copy in halos:
        copy.start()
    to_rows(velocity_ref, edge_ref, v_ref, wide)
    for copy in copies + halos:
        copy.wait()


def fill_rims(ext, cells, before_ref, after_ref):
    margin = before_ref.shape[0]
    ext[cells : cells + margin, :] = before_ref[...].astype(F32)
    ext[cells + margin : cells + 2 * margin, :] = after_ref[...].astype(F32)


def edge_part(levels, ec_ref, v_ref, v_out, ext, dif):
    edges = v_ref.shape[0]

    def some_edges(base):
        place = base + base // LANES * LANES
        found = []
        for u in range(32):
            found.append(row(ext, ec_ref[place + LANES + u]) - row(ext, ec_ref[place + u]))
        for u in range(32):
            dif[pl.ds(base + u, 1), :] = found[u]

    loop(edges, 32, some_edges)

    def move(base):
        at = pl.ds(base, 128)
        v = v_ref[at, :]
        coef = v[:, levels : levels + 1]
        v_out[at, :] = jnp.where(level_mask(levels, v.shape), v - coef * dif[at, :], v)

    loop(edges, 128, move)


def cell_part(ce_ref, moved, beside):
    cells = beside.shape[1]

    def some_cells(base):
        found = []
        for u in range(16):
            for k in range(3):
                found.append((u, k, row(moved, ce_ref[k * cells + base + u])))
        for u, k, value in found:
            beside[k, pl.ds(base + u, 1), :] = value

    loop(cells, 16, some_cells)


def spread_of(levels, h, a0, a1, a2):
    return (
        h[:, levels : levels + 1] * a0
        + h[:, levels + 1 : levels + 2] * a1
        + h[:, levels + 2 : levels + 3] * a2
    )


def first_kernel(
    levels, ec_ref, ce_ref, halo_ref, sb_ref, h_ref, v_ref, before_ref, after_ref, tr_ref,
    h_out, v_out, pack_out, own_ref, other_ref, ext, dif, beside, stage,
):
    cells = h_ref.shape[0]
    ext[0:cells, :] = h_ref[...]
    fill_rims(ext, cells, before_ref, after_ref)
    edge_part(levels, ec_ref, v_ref, v_out, ext, dif)
    cell_part(ce_ref, v_out, beside)
    pad = own_ref.shape[0] // (NDER + tr_ref.shape[0])

    def move(base):
        at = pl.ds(base, 128)
        h = h_ref[at, :]
        div = spread_of(levels, h, beside[0, at, :], beside[1, at, :], beside[2, at, :])
        h_out[at, :] = jnp.where(level_mask(levels, h.shape), h - div, h)

    loop(cells, 128, move)
    pack_rows(halo_ref, h_out, pack_out, stage)
    me = lax.axis_index("stack")
    half = sb_ref.shape[0] // 2
    third = 1.0 / 3.0
    for x_ref in (own_ref, other_ref):
        for t in range(tr_ref.shape[0]):
            end = (NDER + t + 1) * pad
            x_ref[end - 16 : end, :] = jnp.zeros((16, x_ref.shape[1]), BF16)
    for which, x_ref in ((me, own_ref), (1 - me, other_ref)):
        for j in range(half):
            b = jnp.maximum(sb_ref[which * half + j], 0)
            at = pl.ds(pl.multiple_of(b * BLK, BLK), BLK)
            cols = slice(j * BLK, (j + 1) * BLK)
            h, a0, a1, a2 = h_ref[at, :], beside[0, at, :], beside[1, at, :], beside[2, at, :]
            fields = (
                h_out[at, :],
                spread_of(levels, h, a0, a1, a2),
                (a0 * a0 + a1 * a1 + a2 * a2) * third,
                (a0 + a1 + a2) * third,
            )
            for q, field in enumerate(fields):
                x_ref[q * pad : (q + 1) * pad, cols] = field.T[0:pad, :].astype(BF16)
            for t in range(tr_ref.shape[0]):
                q = NDER + t
                x_ref[q * pad : q * pad + levels, cols] = tr_ref[t, :, at]


def by_quantity(w_ref, nq, pad):
    rows, hid = w_ref.shape
    levels = rows // nq
    level = lax.broadcasted_iota(jnp.int32, (pad, rows), 0)
    entry = lax.broadcasted_iota(jnp.int32, (pad, rows), 1)
    parts = []
    for q in range(nq):
        chosen = (entry == level * nq + q) & (level < levels)
        chosen = jnp.where(chosen, 1.0, 0.0).astype(BF16)
        parts.append(jnp.dot(chosen, w_ref[...], preferred_element_type=F32).T)
    return jnp.concatenate(parts, axis=1).astype(BF16)


def second_kernel(sizes, ec_ref, ce_ref, h_ref, v_ref, x_own, x_mine, packed, bias_one, *refs):
    weights, refs = refs[:8], refs[8:]
    out_ref, keep_ref, got_ref, x_other, before, after, send, first, sems, moved, ext, dif, beside = refs
    nq, pad, n_cells, n_role = sizes
    cells = h_ref.shape[0]
    levels = out_ref.shape[0]
    me = lax.axis_index("stack")
    ring = around_ring(n_cells, n_role)
    twin = {"stack": 1 - me}
    greet(ring + [twin])
    halos = halo_copies(packed, before, after, sems, ring)
    swap = remote(x_mine, x_other, sems, 2, twin)
    for copy in halos + [swap]:
        copy.start()
    ours, theirs = weights[:4], weights[4:]
    first[0] = by_quantity(ours[0], nq, pad)
    first[1] = by_quantity(theirs[0], nq, pad)
    ext[0:cells, :] = h_ref[...]
    send[...] = jnp.zeros_like(send)
    for copy in halos:
        copy.wait()
    fill_rims(ext, cells, before, after)
    edge_part(levels, ec_ref, v_ref, moved, ext, dif)
    swap.wait()
    physics((x_own, x_other), first, bias_one, (ours, theirs), keep_ref, send)
    back = remote(send, got_ref, sems, 3, twin)
    back.start()
    cell_part(ce_ref, moved, beside)
    for b in range(cells // BLK):
        at = slice(b * BLK, (b + 1) * BLK)
        h = h_ref[at, :]
        div = spread_of(levels, h, beside[0, at, :], beside[1, at, :], beside[2, at, :])
        out_ref[:, at] = (h - div).T[0:levels, :]
    back.wait()


def physics(inputs, first, bias_one, weights, keep_ref, send_ref):
    me = lax.axis_index("stack")
    x_own, x_other = inputs

    def dot(a, b):
        return jnp.dot(a, b, preferred_element_type=F32)

    def across(a, b):
        return lax.dot_general(a, b, (((0,), (0,)), ((), ())), preferred_element_type=F32)

    def silu(v):
        return (v / (1.0 + jnp.exp(-v))).astype(BF16)

    chunk = 256
    levels = keep_ref.shape[0]
    ones = jnp.ones((1, chunk), BF16)
    for base in range(0, x_own.shape[1], chunk):
        at = slice(base, base + chunk)
        one = dot(first[0], x_own[:, at]) + dot(first[1], x_other[:, at])
        one = silu(one + across(bias_one[...], ones))
        total = None
        for _, second, third, bias in weights:
            two = silu(across(second[...], one) + across(bias[...], ones))
            term = across(third[...], two)
            total = term if total is None else total + term
        low, high = total[0:levels], total[levels : 2 * levels]
        keep_ref[:, at] = jnp.where(me == 0, low, high).astype(BF16).astype(F32)
        send_ref[0:levels, at] = jnp.where(me == 0, high, low).astype(BF16)


def close_kernel(sb_ref, live_ref, wanted_ref, h_ref, keep_ref, got_ref, out_ref):
    levels = h_ref.shape[0]
    slots = sb_ref.shape[0]
    cap = slots // wanted_ref.shape[0]
    here = lax.axis_index("cells") * cap
    me = lax.axis_index("stack")
    half = sb_ref.shape[0] // 2
    out_ref[...] = h_ref[...]
    lane = lax.broadcasted_iota(jnp.int32, (levels, BLK), 1)
    for which, ref in ((me, keep_ref), (1 - me, got_ref)):
        for j in range(half):
            s = which * half + j
            b = jnp.maximum(sb_ref[s], 0)
            at = pl.ds(pl.multiple_of(b * BLK, BLK), BLK)
            tend = ref[:, j * BLK : (j + 1) * BLK].astype(F32)[0:levels, :]
            dest = lax.div(s, cap)
            entry = here + lax.rem(s, cap)
            uses = jnp.int32(0)
            for i in range(wanted_ref.shape[1]):
                uses += (wanted_ref[dest, i] == entry).astype(jnp.int32)
            live = jnp.where((uses > 0) & (sb_ref[s] >= 0), live_ref[b], 0)
            tend = jnp.where(lane < live, tend, 0.0)
            out_ref[:, at] = out_ref[:, at] + tend


def body(
    height, velocity, tracers, edge_coef, cell_coef, halo_send, edge_cells, cell_edges,
    send_block, recv_slot, block_count, w_first, b_first, w_second, b_second, w_third,
):
    n_cells, n_role = lax.axis_size("cells"), lax.axis_size("role")
    levels, cells = height.shape
    edges = velocity.shape[1]
    margin = halo_send.shape[1] // 2
    slots = send_block.shape[1]
    half_slots = slots // 2
    nq = NDER + tracers.shape[0]
    pad = up16(levels + 3)
    feats = nq * pad
    swap = [(0, 1), (1, 0)]
    halo = halo_send.reshape(-1)
    ec = edge_cells.reshape(2, edges // LANES, LANES).transpose(1, 0, 2).reshape(-1)
    ce = cell_edges.reshape(-1)
    sb = send_block.reshape(-1)

    def shape(dims, dtype):
        return jax.ShapeDtypeStruct(dims, dtype)

    ours = (w_first, w_second, w_third, b_second[None])
    theirs = tuple(lax.ppermute(array, "stack", swap) for array in ours)
    halo_shape = shape((margin, LANES), BF16)
    recv = jnp.pad(recv_slot, ((0, 0), (0, LANES - recv_slot.shape[1])), constant_values=-1)
    h_rows, v_rows, before, after, wanted = pl.pallas_call(
        functools.partial(open_kernel, (n_cells, n_role)),
        out_shape=(
            shape((cells, LANES), F32),
            shape((edges, LANES), F32),
            halo_shape,
            halo_shape,
            shape((n_cells, 1, LANES), jnp.int32),
        ),
        in_specs=[SMEM] + [VMEM] * 5,
        out_specs=(VMEM,) * 5,
        scratch_shapes=[
            pltpu.VMEM((LANES, max(cells, edges)), F32),
            pltpu.VMEM((2 * margin, LANES), F32),
            pltpu.VMEM((2 * margin, LANES), BF16),
            pltpu.SemaphoreType.DMA((2, n_cells + 1)),
        ],
        compiler_params=remote_params(0),
        name="open_rows",
    )(halo, height, cell_coef, velocity, edge_coef, recv)
    wanted = wanted[:, 0, : recv_slot.shape[1]]

    field_scratch = [
        pltpu.VMEM((cells + 2 * margin, LANES), F32),
        pltpu.VMEM((edges, LANES), F32),
        pltpu.VMEM((3, cells, LANES), F32),
    ]
    x_shape = shape((feats, half_slots * BLK), BF16)
    h_rows, v_rows, packed, x_own, x_send = pl.pallas_call(
        functools.partial(first_kernel, levels),
        out_shape=(
            shape((cells, LANES), F32),
            shape((edges, LANES), F32),
            shape((2 * margin, LANES), BF16),
            x_shape,
            x_shape,
        ),
        in_specs=[SMEM] * 4 + [VMEM] * 5,
        out_specs=(VMEM,) * 5,
        scratch_shapes=field_scratch + [pltpu.VMEM((2 * margin, LANES), F32)],
        compiler_params=PARAMS,
        name="first_substep",
    )(ec, ce, halo, sb, h_rows, v_rows, before, after, tracers)

    width = half_slots * BLK
    t_shape = shape((pad, width), BF16)
    h_second, keep, got = pl.pallas_call(
        functools.partial(second_kernel, (nq, pad, n_cells, n_role)),
        out_shape=(shape((levels, cells), F32), shape((levels, width), F32), t_shape),
        in_specs=[SMEM] * 2 + [VMEM] * 14,
        out_specs=(VMEM,) * 3,
        scratch_shapes=[
            pltpu.VMEM(x_shape.shape, BF16),
            pltpu.VMEM(halo_shape.shape, BF16),
            pltpu.VMEM(halo_shape.shape, BF16),
            pltpu.VMEM(t_shape.shape, BF16),
            pltpu.VMEM((2, w_first.shape[1], feats), BF16),
            pltpu.SemaphoreType.DMA((2, 4)),
            pltpu.VMEM((edges, LANES), F32),
        ]
        + field_scratch,
        compiler_params=remote_params(1),
        name="second_substep",
    )(ec, ce, h_rows, v_rows, x_own, x_send, packed, b_first[None], *ours, *theirs)

    return pl.pallas_call(
        close_kernel,
        out_shape=shape((levels, cells), F32),
        in_specs=[SMEM] * 3 + [VMEM] * 3,
        out_specs=VMEM,
        compiler_params=PARAMS,
        name="close_add",
    )(sb, block_count.reshape(-1), wanted, h_second, keep, got)


def solution(mesh):
    placed = (
        P("stack", ("groups", "cells", "role")),
        P("stack", ("groups", "cells", "role")),
        P(None, "stack", ("groups", "cells", "role")),
        P(("cells", "role")),
        P(None, ("cells", "role")),
        P(("cells", "role"), None),
        P(("cells", "role"), None, None),
        P(("cells", "role"), None, None),
        P(("cells", "role"), None),
        P(("cells", "role"), None),
        P(("cells", "role"), None),
        P("stack", None),
        P(),
        P(None, "stack"),
        P("stack"),
        P("stack", None),
    )
    return jax.shard_map(
        body,
        mesh=mesh,
        in_specs=placed,
        out_specs=P("stack", ("groups", "cells", "role")),
        check_vma=False,
    )
```

```python
import functools
import jax
import jax.numpy as jnp
from jax import lax
from jax.experimental import pallas as pl
from jax.experimental.pallas import tpu as pltpu
from jax.sharding import PartitionSpec as P

BLK = 128
LANES = 128
NDER = 4
F32 = jnp.float32
BF16 = jnp.bfloat16
VMEM = pl.BlockSpec(memory_space=pltpu.VMEM)
SMEM = pl.BlockSpec(memory_space=pltpu.SMEM)
PARAMS = pltpu.CompilerParams(vmem_limit_bytes=56 * 1024 * 1024)


def remote_params(collective_id):
    return pltpu.CompilerParams(
        vmem_limit_bytes=56 * 1024 * 1024, collective_id=collective_id, has_side_effects=True
    )


def up16(n):
    return -(-n // 16) * 16


def row(ref, i):
    return ref[pl.ds(i, 1), :]


def level_mask(levels, shape):
    return lax.broadcasted_iota(jnp.int32, shape, 1) < levels


def loop(count, step, body):
    def run(i, carry):
        body(pl.multiple_of(i * step, step))
        return carry

    lax.fori_loop(0, count // step, run, 0)


def pack_rows(index_ref, rows_ref, out_ref, stage):
    count = index_ref.shape[0]

    def some(base):
        for u in range(16):
            stage[pl.ds(base + u, 1), :] = row(rows_ref, index_ref[base + u])

    loop(count, 16, some)
    out_ref[...] = stage[...].astype(out_ref.dtype)


def remote(src, dst, sems, at, target):
    return pltpu.make_async_remote_copy(
        src_ref=src,
        dst_ref=dst,
        send_sem=sems.at[0, at],
        recv_sem=sems.at[1, at],
        device_id=target,
        device_id_type=pl.DeviceIdType.MESH,
    )


def greet(targets):
    barrier = pltpu.get_barrier_semaphore()
    for target in targets:
        pl.semaphore_signal(barrier, inc=1, device_id=target, device_id_type=pl.DeviceIdType.MESH)
    pl.semaphore_wait(barrier, len(targets))


def around_ring(n_cells, n_role):
    size = n_cells * n_role
    me = lax.axis_index("cells") * n_role + lax.axis_index("role")
    found = []
    for step in (1, size - 1):
        there = lax.rem(me + step, size)
        found.append({"cells": lax.div(there, n_role), "role": lax.rem(there, n_role)})
    return found


def halo_copies(packed, before, after, sems, ring):
    margin = packed.shape[0] // 2
    return [
        remote(packed.at[pl.ds(margin, margin)], before, sems, 0, ring[0]),
        remote(packed.at[pl.ds(0, margin)], after, sems, 1, ring[1]),
    ]


def to_rows(field_ref, extra_ref, rows_ref, wide):
    levels, count = field_ref.shape
    extra = extra_ref[...].reshape(-1, count)
    wide[0:levels, 0:count] = field_ref[...]
    wide[levels : levels + extra.shape[0], 0:count] = extra
    for b in range(count // BLK):
        cols = slice(b * BLK, (b + 1) * BLK)
        rows_ref[cols, :] = wide[:, cols].T


def open_kernel(
    mesh_size, halo_ref, height_ref, coef_ref, velocity_ref, edge_ref, recv_ref,
    rows_ref, v_ref, before_ref, after_ref, table_ref, wide, stage, packed, sems,
):
    n_cells, n_role = mesh_size
    ring = around_ring(n_cells, n_role)
    me = lax.axis_index("cells")
    peers = [{"cells": lax.rem(me + step, n_cells)} for step in range(1, n_cells)]
    greet(ring + peers)
    copies = [
        remote(recv_ref, table_ref.at[me], sems, 2 + i, peer) for i, peer in enumerate(peers)
    ]
    for copy in copies:
        copy.start()
    table_ref[me] = recv_ref[...]
    wide[...] = jnp.zeros_like(wide)
    to_rows(height_ref, coef_ref, rows_ref, wide)
    pack_rows(halo_ref, rows_ref, packed, stage)
    halos = halo_copies(packed, before_ref, after_ref, sems, ring)
    for copy in halos:
        copy.start()
    to_rows(velocity_ref, edge_ref, v_ref, wide)
    for copy in copies + halos:
        copy.wait()


def fill_rims(ext, cells, before_ref, after_ref):
    margin = before_ref.shape[0]
    ext[cells : cells + margin, :] = before_ref[...].astype(F32)
    ext[cells + margin : cells + 2 * margin, :] = after_ref[...].astype(F32)


def edge_part(levels, ec_ref, v_ref, v_out, ext, dif):
    edges = v_ref.shape[0]

    def some_edges(base):
        place = base + base // LANES * LANES
        found = []
        for u in range(32):
            found.append(row(ext, ec_ref[place + LANES + u]) - row(ext, ec_ref[place + u]))
        for u in range(32):
            dif[pl.ds(base + u, 1), :] = found[u]

    loop(edges, 32, some_edges)

    def move(base):
        at = pl.ds(base, 128)
        v = v_ref[at, :]
        coef = v[:, levels : levels + 1]
        v_out[at, :] = jnp.where(level_mask(levels, v.shape), v - coef * dif[at, :], v)

    loop(edges, 128, move)


def cell_part(ce_ref, moved, beside):
    cells = beside.shape[1]

    def some_cells(base):
        found = []
        for u in range(16):
            for k in range(3):
                found.append((u, k, row(moved, ce_ref[k * cells + base + u])))
        for u, k, value in found:
            beside[k, pl.ds(base + u, 1), :] = value

    loop(cells, 16, some_cells)


def spread_of(levels, h, a0, a1, a2):
    return (
        h[:, levels : levels + 1] * a0
        + h[:, levels + 1 : levels + 2] * a1
        + h[:, levels + 2 : levels + 3] * a2
    )


def first_kernel(
    levels, ec_ref, ce_ref, halo_ref, sb_ref, h_ref, v_ref, before_ref, after_ref, tr_ref,
    h_out, v_out, pack_out, own_ref, other_ref, ext, dif, beside, stage,
):
    cells = h_ref.shape[0]
    ext[0:cells, :] = h_ref[...]
    fill_rims(ext, cells, before_ref, after_ref)
    edge_part(levels, ec_ref, v_ref, v_out, ext, dif)
    cell_part(ce_ref, v_out, beside)
    pad = own_ref.shape[0] // (NDER + tr_ref.shape[0])

    def move(base):
        at = pl.ds(base, 128)
        h = h_ref[at, :]
        div = spread_of(levels, h, beside[0, at, :], beside[1, at, :], beside[2, at, :])
        h_out[at, :] = jnp.where(level_mask(levels, h.shape), h - div, h)

    loop(cells, 128, move)
    pack_rows(halo_ref, h_out, pack_out, stage)
    me = lax.axis_index("stack")
    half = sb_ref.shape[0] // 2
    third = 1.0 / 3.0
    for x_ref in (own_ref, other_ref):
        for t in range(tr_ref.shape[0]):
            end = (NDER + t + 1) * pad
            x_ref[end - 16 : end, :] = jnp.zeros((16, x_ref.shape[1]), BF16)
    for which, x_ref in ((me, own_ref), (1 - me, other_ref)):
        for j in range(half):
            b = jnp.maximum(sb_ref[which * half + j], 0)
            at = pl.ds(pl.multiple_of(b * BLK, BLK), BLK)
            cols = slice(j * BLK, (j + 1) * BLK)
            h, a0, a1, a2 = h_ref[at, :], beside[0, at, :], beside[1, at, :], beside[2, at, :]
            fields = (
                h_out[at, :],
                spread_of(levels, h, a0, a1, a2),
                (a0 * a0 + a1 * a1 + a2 * a2) * third,
                (a0 + a1 + a2) * third,
            )
            for q, field in enumerate(fields):
                x_ref[q * pad : (q + 1) * pad, cols] = field.T[0:pad, :].astype(BF16)
            for t in range(tr_ref.shape[0]):
                q = NDER + t
                x_ref[q * pad : q * pad + levels, cols] = tr_ref[t, :, at]


def by_quantity(w_ref, nq, pad):
    rows, hid = w_ref.shape
    levels = rows // nq
    level = lax.broadcasted_iota(jnp.int32, (pad, rows), 0)
    entry = lax.broadcasted_iota(jnp.int32, (pad, rows), 1)
    parts = []
    for q in range(nq):
        chosen = (entry == level * nq + q) & (level < levels)
        chosen = jnp.where(chosen, 1.0, 0.0).astype(BF16)
        parts.append(jnp.dot(chosen, w_ref[...], preferred_element_type=F32).T)
    return jnp.concatenate(parts, axis=1).astype(BF16)


def second_kernel(sizes, ec_ref, ce_ref, h_ref, v_ref, x_own, x_mine, packed, bias_one, *refs):
    weights, refs = refs[:8], refs[8:]
    out_ref, keep_ref, got_ref, x_other, before, after, send, first, sems, moved, ext, dif, beside = refs
    nq, pad, n_cells, n_role = sizes
    cells = h_ref.shape[0]
    levels = out_ref.shape[0]
    me = lax.axis_index("stack")
    ring = around_ring(n_cells, n_role)
    twin = {"stack": 1 - me}
    greet(ring + [twin])
    halos = halo_copies(packed, before, after, sems, ring)
    swap = remote(x_mine, x_other, sems, 2, twin)
    for copy in halos + [swap]:
        copy.start()
    ours, theirs = weights[:4], weights[4:]
    first[0] = by_quantity(ours[0], nq, pad)
    first[1] = by_quantity(theirs[0], nq, pad)
    ext[0:cells, :] = h_ref[...]
    send[...] = jnp.zeros_like(send)
    for copy in halos:
        copy.wait()
    fill_rims(ext, cells, before, after)
    edge_part(levels, ec_ref, v_ref, moved, ext, dif)
    swap.wait()
    physics((x_own, x_other), first, bias_one, (ours, theirs), keep_ref, send)
    back = remote(send, got_ref, sems, 3, twin)
    back.start()
    cell_part(ce_ref, moved, beside)
    for b in range(cells // BLK):
        at = slice(b * BLK, (b + 1) * BLK)
        h = h_ref[at, :]
        div = spread_of(levels, h, beside[0, at, :], beside[1, at, :], beside[2, at, :])
        out_ref[:, at] = (h - div).T[0:levels, :]
    back.wait()


def physics(inputs, first, bias_one, weights, keep_ref, send_ref):
    me = lax.axis_index("stack")
    x_own, x_other = inputs

    def dot(a, b):
        return jnp.dot(a, b, preferred_element_type=F32)

    def across(a, b):
        return lax.dot_general(a, b, (((0,), (0,)), ((), ())), preferred_element_type=F32)

    def silu(v):
        return (v / (1.0 + jnp.exp(-v))).astype(BF16)

    chunk = x_own.shape[1]
    levels = keep_ref.shape[0]
    ones = jnp.ones((1, chunk), BF16)
    for base in range(0, x_own.shape[1], chunk):
        at = slice(base, base + chunk)
        one = dot(first[0], x_own[:, at]) + dot(first[1], x_other[:, at])
        one = silu(one + across(bias_one[...], ones))
        total = None
        for _, second, third, bias in weights:
            two = silu(across(second[...], one) + across(bias[...], ones))
            term = across(third[...], two)
            total = term if total is None else total + term
        low, high = total[0:levels], total[levels : 2 * levels]
        keep_ref[:, at] = jnp.where(me == 0, low, high).astype(BF16).astype(F32)
        send_ref[0:levels, at] = jnp.where(me == 0, high, low).astype(BF16)


def close_kernel(sb_ref, live_ref, wanted_ref, h_ref, keep_ref, got_ref, out_ref):
    levels = h_ref.shape[0]
    slots = sb_ref.shape[0]
    cap = slots // wanted_ref.shape[0]
    here = lax.axis_index("cells") * cap
    me = lax.axis_index("stack")
    half = sb_ref.shape[0] // 2
    out_ref[...] = h_ref[...]
    lane = lax.broadcasted_iota(jnp.int32, (levels, BLK), 1)
    for which, ref in ((me, keep_ref), (1 - me, got_ref)):
        for j in range(half):
            s = which * half + j
            b = jnp.maximum(sb_ref[s], 0)
            at = pl.ds(pl.multiple_of(b * BLK, BLK), BLK)
            tend = ref[:, j * BLK : (j + 1) * BLK].astype(F32)[0:levels, :]
            dest = lax.div(s, cap)
            entry = here + lax.rem(s, cap)
            uses = jnp.int32(0)
            for i in range(wanted_ref.shape[1]):
                uses += (wanted_ref[dest, i] == entry).astype(jnp.int32)
            live = jnp.where((uses > 0) & (sb_ref[s] >= 0), live_ref[b], 0)
            tend = jnp.where(lane < live, tend, 0.0)
            out_ref[:, at] = out_ref[:, at] + tend


def body(
    height, velocity, tracers, edge_coef, cell_coef, halo_send, edge_cells, cell_edges,
    send_block, recv_slot, block_count, w_first, b_first, w_second, b_second, w_third,
):
    n_cells, n_role = lax.axis_size("cells"), lax.axis_size("role")
    levels, cells = height.shape
    edges = velocity.shape[1]
    margin = halo_send.shape[1] // 2
    slots = send_block.shape[1]
    half_slots = slots // 2
    nq = NDER + tracers.shape[0]
    pad = up16(levels + 3)
    feats = nq * pad
    swap = [(0, 1), (1, 0)]
    halo = halo_send.reshape(-1)
    ec = edge_cells.reshape(2, edges // LANES, LANES).transpose(1, 0, 2).reshape(-1)
    ce = cell_edges.reshape(-1)
    sb = send_block.reshape(-1)

    def shape(dims, dtype):
        return jax.ShapeDtypeStruct(dims, dtype)

    ours = (w_first, w_second, w_third, b_second[None])
    theirs = tuple(lax.ppermute(array, "stack", swap) for array in ours)
    halo_shape = shape((margin, LANES), BF16)
    recv = jnp.pad(recv_slot, ((0, 0), (0, LANES - recv_slot.shape[1])), constant_values=-1)
    h_rows, v_rows, before, after, wanted = pl.pallas_call(
        functools.partial(open_kernel, (n_cells, n_role)),
        out_shape=(
            shape((cells, LANES), F32),
            shape((edges, LANES), F32),
            halo_shape,
            halo_shape,
            shape((n_cells, 1, LANES), jnp.int32),
        ),
        in_specs=[SMEM] + [VMEM] * 5,
        out_specs=(VMEM,) * 5,
        scratch_shapes=[
            pltpu.VMEM((LANES, max(cells, edges)), F32),
            pltpu.VMEM((2 * margin, LANES), F32),
            pltpu.VMEM((2 * margin, LANES), BF16),
            pltpu.SemaphoreType.DMA((2, n_cells + 1)),
        ],
        compiler_params=remote_params(0),
        name="open_rows",
    )(halo, height, cell_coef, velocity, edge_coef, recv)
    wanted = wanted[:, 0, : recv_slot.shape[1]]

    field_scratch = [
        pltpu.VMEM((cells + 2 * margin, LANES), F32),
        pltpu.VMEM((edges, LANES), F32),
        pltpu.VMEM((3, cells, LANES), F32),
    ]
    x_shape = shape((feats, half_slots * BLK), BF16)
    h_rows, v_rows, packed, x_own, x_send = pl.pallas_call(
        functools.partial(first_kernel, levels),
        out_shape=(
            shape((cells, LANES), F32),
            shape((edges, LANES), F32),
            shape((2 * margin, LANES), BF16),
            x_shape,
            x_shape,
        ),
        in_specs=[SMEM] * 4 + [VMEM] * 5,
        out_specs=(VMEM,) * 5,
        scratch_shapes=field_scratch + [pltpu.VMEM((2 * margin, LANES), F32)],
        compiler_params=PARAMS,
        name="first_substep",
    )(ec, ce, halo, sb, h_rows, v_rows, before, after, tracers)

    width = half_slots * BLK
    t_shape = shape((pad, width), BF16)
    h_second, keep, got = pl.pallas_call(
        functools.partial(second_kernel, (nq, pad, n_cells, n_role)),
        out_shape=(shape((levels, cells), F32), shape((levels, width), F32), t_shape),
        in_specs=[SMEM] * 2 + [VMEM] * 14,
        out_specs=(VMEM,) * 3,
        scratch_shapes=[
            pltpu.VMEM(x_shape.shape, BF16),
            pltpu.VMEM(halo_shape.shape, BF16),
            pltpu.VMEM(halo_shape.shape, BF16),
            pltpu.VMEM(t_shape.shape, BF16),
            pltpu.VMEM((2, w_first.shape[1], feats), BF16),
            pltpu.SemaphoreType.DMA((2, 4)),
            pltpu.VMEM((edges, LANES), F32),
        ]
        + field_scratch,
        compiler_params=remote_params(1),
        name="second_substep",
    )(ec, ce, h_rows, v_rows, x_own, x_send, packed, b_first[None], *ours, *theirs)

    return pl.pallas_call(
        close_kernel,
        out_shape=shape((levels, cells), F32),
        in_specs=[SMEM] * 3 + [VMEM] * 3,
        out_specs=VMEM,
        compiler_params=PARAMS,
        name="close_add",
    )(sb, block_count.reshape(-1), wanted, h_second, keep, got)


def solution(mesh):
    placed = (
        P("stack", ("groups", "cells", "role")),
        P("stack", ("groups", "cells", "role")),
        P(None, "stack", ("groups", "cells", "role")),
        P(("cells", "role")),
        P(None, ("cells", "role")),
        P(("cells", "role"), None),
        P(("cells", "role"), None, None),
        P(("cells", "role"), None, None),
        P(("cells", "role"), None),
        P(("cells", "role"), None),
        P(("cells", "role"), None),
        P("stack", None),
        P(),
        P(None, "stack"),
        P("stack"),
        P("stack", None),
    )
    return jax.shard_map(
        body,
        mesh=mesh,
        in_specs=placed,
        out_specs=P("stack", ("groups", "cells", "role")),
        check_vma=False,
    )
```
